32 devices in a mesh: groups: 2 (over y), depth: 4 (over z), dp: 2 (over x), sub: 2 (over core).
Axes of the slice: x: 2, y: 2, z: 4, core: 2. Of those that a mesh axis runs over, the one named last changes fastest.
Arguments:
- objects: float32 [16, 2, 512, 512], P(('groups', 'depth'), None, 'sub'), parts along dimension 0, may hold values from -1.1 to 1.1, as said below
- probe_wave: float32 [2, 256, 256], replicated, may hold values from -6 to 6
- offsets: int32 [32, 2], P(('groups', 'dp', 'sub')), parts along dimension 0, may hold values from 0 to 256
- counts: int32 [32, 256, 256], P(('groups', 'dp', 'sub')), parts along dimension 0, may hold values from 0 to 7
Outputs:
- object_grad: float32 [16, 2, 512, 512], P(('groups', 'depth'), None, ('dp', 'sub')), parts along dimension 0
The draws below stay inside these ranges and needn't reach their ends.
There are 2 independent parts, one for each index of `groups`. The reference program is written for one: setup_inputs(seed, part) draws one part's arguments, and reference() takes and returns one part's arrays. A program takes and returns all parts, laid end to end along the dimension named above; an argument that names none is the same for every part. Nothing has to cross between parts.
Inputs may be any that keep to these rules, and one draw needn't show every extreme that they name: The pair objects[k,0,r,c], objects[k,1,r,c] has magnitude between 0.8 and 1.1.
All inputs are finite; a program needn't handle non-finite values.
Results may differ from the reference program's by a relative error of at most 0.0003.
Values sent between devices are 32-bit elements; how exact they have to be, the bound alone decides.
A program may use at most 128 MiB of HBM per device.

```python
import jax
import jax.numpy as jnp
from jax import lax

WIN = 256
OBJ = 512
NS = 8
POS = 16


def draw_objects(key, part):
    key_angle, key_magnitude = jax.random.split(jax.random.fold_in(key, 11))
    argument = jax.random.uniform(key_angle, (NS, OBJ, OBJ), jnp.float32, -jnp.pi, jnp.pi)
    magnitude = jax.random.uniform(key_magnitude, (NS, OBJ, OBJ), jnp.float32, 0.85, 1.05)
    return jnp.stack([magnitude * jnp.cos(argument), magnitude * jnp.sin(argument)], axis=1)


def touch_ends(entries, own_key, low, largest):
    extent = entries.shape
    index_at = [jax.random.randint(jax.random.fold_in(own_key, axis), (), 0, extent[axis]) for axis in range(len(extent))]
    entries = entries.at[tuple(index_at)].set(low)
    longest = extent.index(max(extent))
    index_at[longest] = (index_at[longest] + 1) % extent[longest]
    return entries.at[tuple(index_at)].set(largest)


def centred(rng, extent, width, reach, kind=jnp.bfloat16):
    return jnp.clip(width * jax.random.normal(rng, extent, jnp.float32), -reach, reach).astype(kind)


def setup_inputs(seed: int = 0, part: int = 0) -> dict:
    streams_of = jax.random.split(jax.random.key(seed), 5)
    own_keys = jax.random.split(jax.random.fold_in(streams_of[4], part), 5)
    objects = draw_objects(jax.random.fold_in(jax.random.fold_in(streams_of[4], part), 71), part)
    probe_wave = centred(streams_of[1], (2, WIN, WIN), 1.0, 6.0, jnp.float32)
    offsets = touch_ends(jax.random.randint(own_keys[2], (POS, 2), 0, OBJ - WIN + 1), jax.random.fold_in(own_keys[2], 1), 0, OBJ - WIN).astype(jnp.int32)
    counts = touch_ends(jax.random.randint(own_keys[3], (POS, WIN, WIN), 0, 8), jax.random.fold_in(own_keys[3], 1), 0, 7).astype(jnp.int32)
    return {"objects": objects, "probe_wave": probe_wave, "offsets": offsets, "counts": counts}


KAPPA = 40.0

def propagator(window_size, dtype):
    freq_index = jnp.arange(window_size, dtype=jnp.int32)
    frequency = jnp.where(freq_index < window_size // 2, freq_index, freq_index - window_size).astype(dtype) / window_size
    phase_angle = -KAPPA * (frequency[:, None] ** 2 + frequency[None, :] ** 2)
    return jnp.cos(phase_angle) + 1j * jnp.sin(phase_angle)

def reference(objects, probe_wave, offsets, counts):
    kernel_map = propagator(WIN, objects.dtype)
    start_wave = probe_wave[0] + 1j * probe_wave[1]

    def position_loss(object_stack, offset_pair, count_map):

        def slice_step(wave_now, object_slab):
            window = lax.dynamic_slice(object_slab, (jnp.int32(0), offset_pair[0], offset_pair[1]), (2, WIN, WIN))
            wave_now = wave_now * (window[0] + 1j * window[1])
            wave_now = jnp.fft.ifft2(kernel_map * jnp.fft.fft2(wave_now))
            return (wave_now, None)
        wave_end, _ = lax.scan(slice_step, start_wave, object_stack)
        far_field = jnp.fft.fft2(wave_end) / WIN
        residual = jnp.real(far_field) ** 2 + jnp.imag(far_field) ** 2 - 0.25 * count_map.astype(object_stack.dtype)
        return 0.25 * jnp.sum(residual * residual)

    def total_loss(object_stack):

        def accumulate(loss_sum, entry):
            offset_pair, count_map = entry
            return (loss_sum + position_loss(object_stack, offset_pair, count_map), None)
        loss_sum, _ = lax.scan(accumulate, jnp.zeros((), object_stack.dtype), (offsets, counts))
        return loss_sum
    _, pullback = jax.vjp(total_loss, objects)
    return pullback(jnp.ones((), objects.dtype))[0]
```

```python
import functools

import jax
import jax.numpy as jnp
import numpy as np
from jax import lax
from jax.experimental import pallas as pl
from jax.experimental.pallas import tpu as pltpu
from jax.sharding import PartitionSpec as P

KAPPA = 40.0
MESH = pl.DeviceIdType.MESH


def split_tables(matrix):
    real, imag = matrix.real, matrix.imag
    right = np.block([[real, imag], [-imag, real]]).astype(np.float32)
    tables = []
    for block in (right, right.T):
        high = block.astype(jnp.bfloat16)
        low = (block - high.astype(np.float32)).astype(jnp.bfloat16)
        tables += [high, low]
    return np.stack(tables)


def constants(size):
    index = np.arange(size)
    fourier = np.exp(-2j * np.pi * (index[:, None] * index[None, :] % size) / size)
    frequency = np.where(index < size // 2, index, index - size) / size
    ramp = np.exp(-1j * KAPPA * frequency**2)
    circulant = np.conj(fourier) @ (ramp[:, None] * fourier) / size
    circulant = 0.5 * (circulant + circulant.T)
    return split_tables(circulant), split_tables(fourier / np.sqrt(size))


def two_terms(value):
    high = value.astype(jnp.bfloat16)
    low = (value - high.astype(jnp.float32)).astype(jnp.bfloat16)
    return high, low


def dot(left, right):
    return jnp.dot(left, right, preferred_element_type=jnp.float32)


def rows_up(value, shift):
    tiles = value.reshape(value.shape[0] // 8, 8, value.shape[1])
    turned = pltpu.roll(tiles, lax.rem(8 - shift, 8), 1)
    place = lax.broadcasted_iota(jnp.int32, turned[1:].shape, 1)
    moved = jnp.where(place < 8 - shift, turned[:-1], turned[1:])
    return moved.reshape(value.shape[0] - 8, value.shape[1])


def both_sides(real, imag, table):
    size = real.shape[0]
    high, low = two_terms(jnp.concatenate([real, imag], axis=1))
    rows = dot(high, table[0]) + dot(low, table[0]) + dot(high, table[1])
    high, low = two_terms(jnp.concatenate([rows[:, :size], rows[:, size:]], axis=0))
    both = dot(table[2], high) + dot(table[2], low) + dot(table[3], high)
    return both[:size], both[size:]


def greet(neighbours):
    barrier = pltpu.get_barrier_semaphore()
    for axis, index in neighbours:
        pl.semaphore_signal(barrier, inc=1, device_id={axis: index}, device_id_type=MESH)
    pl.semaphore_wait(barrier, len(neighbours))


def others(axis, count):
    me = lax.axis_index(axis)
    return [(axis, lax.rem(me + shift, count)) for shift in range(1, count)]


def gather_kernel(sub_n, objects, full, send, recv, own_sem):
    sub = lax.axis_index("sub")
    layers, _, half, _ = objects.shape
    greet(others("sub", sub_n))
    mine = pl.ds(pl.multiple_of(sub * half, half), half)
    copies = []
    for shift in range(1, sub_n):
        copy = pltpu.make_async_remote_copy(
            src_ref=objects,
            dst_ref=full.at[:, :, mine],
            send_sem=send.at[shift],
            recv_sem=recv.at[shift],
            device_id={"sub": lax.rem(sub + shift, sub_n)},
            device_id_type=MESH,
        )
        copy.start()
        copies.append(copy)
    own = pltpu.make_async_copy(objects, full.at[:, :, mine], own_sem)
    own.start()
    own.wait()
    for copy in copies:
        copy.wait()


def window_kernel(offsets, full, win):
    positions, layers, _, size, _ = win.shape
    width = full.shape[3]

    @pl.loop(0, positions)
    def _(item):
        row, column = offsets[item, 0], offsets[item, 1]
        row_rest = lax.rem(row, 8)
        row_tile = pl.multiple_of(row - row_rest, 8)
        turn = lax.rem(width - column, width)
        for layer in range(layers):
            for part in range(2):
                strip = full[layer, part, pl.ds(row_tile, size), :]
                last = jnp.minimum(row_tile + size, full.shape[2] - 8)
                tail = full[layer, part, pl.ds(pl.multiple_of(last, 8), 8), :]
                strip = pltpu.roll(jnp.concatenate([strip, tail], axis=0), turn, 1)[:, :size]
                win[item, layer, part] = rows_up(strip, row_rest)


def scatter_kernel(offsets, delta, grad):
    positions, layers, _, size, _ = delta.shape
    width = grad.shape[3]
    grad[...] = jnp.zeros_like(grad)

    @pl.loop(0, positions)
    def _(item):
        row, column = offsets[item, 0], offsets[item, 1]
        row_rest = lax.rem(row, 8)
        row_tile = pl.multiple_of(row - row_rest, 8)
        ends = jnp.zeros((8, size), jnp.float32)
        side_by = jnp.zeros((size + 8, width - size), jnp.float32)
        for layer in range(layers):
            for part in range(2):
                tall = jnp.concatenate([ends, delta[item, layer, part], ends], axis=0)
                wide = jnp.concatenate([rows_up(tall, 8 - row_rest), side_by], axis=1)
                grad[layer, part, pl.ds(row_tile, size + 8), :] += pltpu.roll(wide, column, 1)


def sum_kernel(dp_n, sub_n, grad, out, rsub, acc, rdp, s_send, s_recv, d_send, d_recv):
    dp, sub = lax.axis_index("dp"), lax.axis_index("sub")
    layers, _, rows, _ = out.shape
    greet(others("sub", sub_n) + others("dp", dp_n))
    sub_copies = []
    for layer in range(layers):
        group = []
        for shift in range(1, sub_n):
            other = lax.rem(sub + shift, sub_n)
            for chip in range(dp_n):
                start = pl.multiple_of((chip * sub_n + other) * rows, rows)
                copy = pltpu.make_async_remote_copy(
                    src_ref=grad.at[layer, :, pl.ds(start, rows)],
                    dst_ref=rsub.at[layer, shift, chip],
                    send_sem=s_send.at[layer, shift, chip],
                    recv_sem=s_recv.at[layer, shift, chip],
                    device_id={"sub": other},
                    device_id_type=MESH,
                )
                copy.start()
                group.append(copy)
        sub_copies.append(group)
    dp_copies = []
    for layer, group in enumerate(sub_copies):
        for copy in group:
            copy.wait()
        for chip in range(dp_n):
            start = pl.multiple_of((chip * sub_n + sub) * rows, rows)
            total = grad[layer, :, pl.ds(start, rows), :]
            for shift in range(1, sub_n):
                total = total + rsub[layer, shift, chip]
            acc[layer, chip] = total
        group = []
        for shift in range(1, dp_n):
            other = lax.rem(dp + shift, dp_n)
            copy = pltpu.make_async_remote_copy(
                src_ref=acc.at[layer, other],
                dst_ref=rdp.at[layer, shift],
                send_sem=d_send.at[layer, shift],
                recv_sem=d_recv.at[layer, shift],
                device_id={"dp": other},
                device_id_type=MESH,
            )
            copy.start()
            group.append(copy)
        dp_copies.append(group)
    for layer, group in enumerate(dp_copies):
        for copy in group:
            copy.wait()
        total = acc[layer, dp]
        for shift in range(1, dp_n):
            total = total + rdp[layer, shift]
        out[layer] = total


def wave_kernel(
    depth_n, win, probe, counts, prop_table, far_table, delta,
    fin, mid, fout, bin_, bout, f_send, f_recv, b_send, b_recv,
):
    depth = lax.axis_index("depth")
    positions, layers, _, size, _ = win.shape
    is_first, is_last = depth == 0, depth == depth_n - 1
    following = lax.rem(depth + 1, depth_n)
    previous = lax.rem(depth + depth_n - 1, depth_n)
    greet([("depth", following), ("depth", previous)])

    def forward_copy(item):
        return pltpu.make_async_remote_copy(
            src_ref=fout.at[item],
            dst_ref=fin.at[item],
            send_sem=f_send.at[item],
            recv_sem=f_recv.at[item],
            device_id={"depth": following},
            device_id_type=MESH,
        )

    def backward_copy(item):
        return pltpu.make_async_remote_copy(
            src_ref=bout.at[item],
            dst_ref=bin_.at[item],
            send_sem=b_send.at[item],
            recv_sem=b_recv.at[item],
            device_id={"depth": previous},
            device_id_type=MESH,
        )

    def forward(item):
        @pl.when(is_first)
        def _():
            fin[item] = probe[...]

        @pl.when(jnp.logical_not(is_first))
        def _():
            forward_copy(item).wait_recv()

        real, imag = fin[item, 0], fin[item, 1]
        for layer in range(layers):
            if layer > 0:
                mid[item, layer - 1, 0] = real
                mid[item, layer - 1, 1] = imag
            obj_re, obj_im = win[item, layer, 0], win[item, layer, 1]
            real, imag = both_sides(
                real * obj_re - imag * obj_im, real * obj_im + imag * obj_re, prop_table
            )
        fout[item, 0] = real
        fout[item, 1] = imag

        @pl.when(jnp.logical_not(is_last))
        def _():
            forward_copy(item).start()

        @pl.when(is_last)
        def _():
            far_re, far_im = both_sides(fout[item, 0], fout[item, 1], far_table)
            residual = far_re * far_re + far_im * far_im - 0.25 * counts[item].astype(jnp.float32)
            back_re, back_im = both_sides(residual * far_re, -residual * far_im, far_table)
            bin_[item, 0] = back_re
            bin_[item, 1] = back_im

    def backward(item):
        @pl.when(jnp.logical_not(is_last))
        def _():
            backward_copy(item).wait_recv()

        real, imag = bin_[item, 0], bin_[item, 1]
        for layer in reversed(range(layers)):
            real, imag = both_sides(real, imag, prop_table)
            if layer > 0:
                wave_re, wave_im = mid[item, layer - 1, 0], mid[item, layer - 1, 1]
            else:
                wave_re, wave_im = fin[item, 0], fin[item, 1]
            delta[item, layer, 0] = wave_re * real - wave_im * imag
            delta[item, layer, 1] = -(wave_re * imag + wave_im * real)
            obj_re, obj_im = win[item, layer, 0], win[item, layer, 1]
            real, imag = real * obj_re - imag * obj_im, real * obj_im + imag * obj_re

        @pl.when(jnp.logical_not(is_first))
        def _():
            bout[item, 0] = real
            bout[item, 1] = imag
            backward_copy(item).start()

    lag = 2 * (depth_n - 1 - depth)

    @pl.loop(0, positions + 2 * (depth_n - 1))
    def _(step):
        @pl.when(step < positions)
        def _():
            forward(step)

        item = step - lag

        @pl.when((item >= 0) & (item < positions))
        def _():
            backward(item)

    @pl.when(jnp.logical_not(is_last))
    def _():
        @pl.loop(0, positions)
        def _(item):
            forward_copy(item).wait_send()

    @pl.when(jnp.logical_not(is_first))
    def _():
        @pl.loop(0, positions)
        def _(item):
            backward_copy(item).wait_send()


def call(body, shape, in_specs, scratch=(), collective=None):
    extra = {} if collective is None else {"collective_id": collective, "has_side_effects": True}
    return pl.pallas_call(
        body,
        out_shape=jax.ShapeDtypeStruct(shape, jnp.float32),
        in_specs=in_specs,
        out_specs=pl.BlockSpec(memory_space=pltpu.VMEM),
        scratch_shapes=list(scratch),
        compiler_params=pltpu.CompilerParams(vmem_limit_bytes=40 * 1024 * 1024, **extra),
    )


def shards(sizes, objects, probe_wave, offsets, counts):
    depth_n, dp_n, sub_n = sizes
    layers, _, half, width = objects.shape
    side = half * sub_n
    positions, size = counts.shape[0], counts.shape[1]
    rows = side // (dp_n * sub_n)
    prop_table, far_table = constants(size)
    vmem = pl.BlockSpec(memory_space=pltpu.VMEM)
    smem = pl.BlockSpec(memory_space=pltpu.SMEM)
    dma = pltpu.SemaphoreType.DMA

    def block(*shape):
        return pltpu.VMEM(shape, jnp.float32)

    full = call(
        functools.partial(gather_kernel, sub_n),
        (layers, 2, side, width),
        [vmem],
        [dma((sub_n,)), dma((sub_n,)), dma],
        0,
    )(objects)
    windows = (positions, layers, 2, size, size)
    win = call(window_kernel, windows, [smem, vmem])(offsets, full)
    waves = (positions, 2, size, size)
    delta = call(
        functools.partial(wave_kernel, depth_n),
        windows,
        [vmem] * 5,
        [
            block(*waves),
            block(positions, max(layers - 1, 1), 2, size, size),
            block(*waves),
            block(*waves),
            block(*waves),
        ]
        + [dma((positions,))] * 4,
        1,
    )(win, probe_wave, counts, jnp.asarray(prop_table), jnp.asarray(far_table))
    grad = call(scatter_kernel, (layers, 2, side + 8, width), [smem, vmem])(offsets, delta)
    return call(
        functools.partial(sum_kernel, dp_n, sub_n),
        (layers, 2, rows, width),
        [vmem],
        [
            block(layers, sub_n, dp_n, 2, rows, width),
            block(layers, dp_n, 2, rows, width),
            block(layers, dp_n, 2, rows, width),
            dma((layers, sub_n, dp_n)),
            dma((layers, sub_n, dp_n)),
            dma((layers, dp_n)),
            dma((layers, dp_n)),
        ],
        2,
    )(grad)


def solution(mesh):
    placed = (
        P(("groups", "depth"), None, "sub", None),
        P(),
        P(("groups", "dp", "sub"), None),
        P(("groups", "dp", "sub"), None, None),
    )
    sizes = tuple(mesh.shape[axis] for axis in ("depth", "dp", "sub"))
    return jax.shard_map(
        functools.partial(shards, sizes),
        mesh=mesh,
        in_specs=placed,
        out_specs=P(("groups", "depth"), None, ("dp", "sub"), None),
        check_vma=False,
    )
```

```python
import functools

import jax
import jax.numpy as jnp
import numpy as np
from jax import lax
from jax.experimental import pallas as pl
from jax.experimental.pallas import tpu as pltpu
from jax.sharding import PartitionSpec as P

KAPPA = 40.0
MESH = pl.DeviceIdType.MESH


def split_tables(matrix):
    real, imag = matrix.real, matrix.imag
    right = np.block([[real, imag], [-imag, real]]).astype(np.float32)
    tables = []
    for block in (right, right.T):
        high = block.astype(jnp.bfloat16)
        low = (block - high.astype(np.float32)).astype(jnp.bfloat16)
        tables += [high, low]
    return np.stack(tables)


def constants(size):
    index = np.arange(size)
    fourier = np.exp(-2j * np.pi * (index[:, None] * index[None, :] % size) / size)
    frequency = np.where(index < size // 2, index, index - size) / size
    ramp = np.exp(-1j * KAPPA * frequency**2)
    circulant = np.conj(fourier) @ (ramp[:, None] * fourier) / size
    circulant = 0.5 * (circulant + circulant.T)
    return split_tables(circulant), split_tables(fourier / np.sqrt(size))


def two_terms(value):
    high = value.astype(jnp.bfloat16)
    low = (value - high.astype(jnp.float32)).astype(jnp.bfloat16)
    return high, low


def dot(left, right):
    return jnp.dot(left, right, preferred_element_type=jnp.float32)


def rows_up(value, shift):
    tiles = value.reshape(value.shape[0] // 8, 8, value.shape[1])
    turned = pltpu.roll(tiles, lax.rem(8 - shift, 8), 1)
    place = lax.broadcasted_iota(jnp.int32, turned[1:].shape, 1)
    moved = jnp.where(place < 8 - shift, turned[:-1], turned[1:])
    return moved.reshape(value.shape[0] - 8, value.shape[1])


def both_sides(real, imag, table):
    size = real.shape[0]
    high, low = two_terms(jnp.concatenate([real, imag], axis=1))
    rows = dot(high, table[0]) + dot(low, table[0]) + dot(high, table[1])
    high, low = two_terms(jnp.concatenate([rows[:, :size], rows[:, size:]], axis=0))
    both = dot(table[2], high) + dot(table[2], low) + dot(table[3], high)
    return both[:size], both[size:]


def greet(neighbours):
    barrier = pltpu.get_barrier_semaphore()
    for axis, index in neighbours:
        pl.semaphore_signal(barrier, inc=1, device_id={axis: index}, device_id_type=MESH)
    pl.semaphore_wait(barrier, len(neighbours))


def others(axis, count):
    me = lax.axis_index(axis)
    return [(axis, lax.rem(me + shift, count)) for shift in range(1, count)]


def gather_kernel(sub_n, objects, full, send, recv, own_sem):
    sub = lax.axis_index("sub")
    layers, _, half, _ = objects.shape
    greet(others("sub", sub_n))
    mine = pl.ds(pl.multiple_of(sub * half, half), half)
    copies = []
    for shift in range(1, sub_n):
        copy = pltpu.make_async_remote_copy(
            src_ref=objects,
            dst_ref=full.at[:, :, mine],
            send_sem=send.at[shift],
            recv_sem=recv.at[shift],
            device_id={"sub": lax.rem(sub + shift, sub_n)},
            device_id_type=MESH,
        )
        copy.start()
        copies.append(copy)
    own = pltpu.make_async_copy(objects, full.at[:, :, mine], own_sem)
    own.start()
    own.wait()
    for copy in copies:
        copy.wait()


def window_kernel(offsets, full, win):
    positions, layers, _, size, _ = win.shape
    width = full.shape[3]

    @pl.loop(0, positions)
    def _(item):
        row, column = offsets[item, 0], offsets[item, 1]
        row_rest = lax.rem(row, 8)
        row_tile = pl.multiple_of(row - row_rest, 8)
        turn = lax.rem(width - column, width)
        for layer in range(layers):
            for part in range(2):
                strip = full[layer, part, pl.ds(row_tile, size), :]
                last = jnp.minimum(row_tile + size, full.shape[2] - 8)
                tail = full[layer, part, pl.ds(pl.multiple_of(last, 8), 8), :]
                strip = pltpu.roll(jnp.concatenate([strip, tail], axis=0), turn, 1)[:, :size]
                win[item, layer, part] = rows_up(strip, row_rest)


def scatter_kernel(offsets, delta, grad):
    positions, layers, _, size, _ = delta.shape
    width = grad.shape[3]
    grad[...] = jnp.zeros_like(grad)

    @pl.loop(0, positions)
    def _(item):
        row, column = offsets[item, 0], offsets[item, 1]
        row_rest = lax.rem(row, 8)
        row_tile = pl.multiple_of(row - row_rest, 8)
        ends = jnp.zeros((8, size), jnp.float32)
        side_by = jnp.zeros((size + 8, width - size), jnp.float32)
        for layer in range(layers):
            for part in range(2):
                tall = jnp.concatenate([ends, delta[item, layer, part], ends], axis=0)
                wide = jnp.concatenate([rows_up(tall, 8 - row_rest), side_by], axis=1)
                grad[layer, part, pl.ds(row_tile, size + 8), :] += pltpu.roll(wide, column, 1)


def sum_kernel(dp_n, sub_n, grad, out, rsub, acc, rdp, s_send, s_recv, d_send, d_recv):
    dp, sub = lax.axis_index("dp"), lax.axis_index("sub")
    layers, _, rows, _ = out.shape
    greet(others("sub", sub_n) + others("dp", dp_n))
    pieces = [(layer, part) for layer in range(layers) for part in range(2)]

    def sub_copy(layer, part, hop, shift):
        other = lax.rem(sub + shift, sub_n)
        chip = lax.rem(dp + hop, dp_n)
        start = pl.multiple_of((chip * sub_n + other) * rows, rows)
        return pltpu.make_async_remote_copy(
            src_ref=grad.at[layer, part, pl.ds(start, rows)],
            dst_ref=rsub.at[layer, part, hop, shift],
            send_sem=s_send.at[layer, part, hop, shift],
            recv_sem=s_recv.at[layer, part, hop, shift],
            device_id={"sub": other},
            device_id_type=MESH,
        )

    def dp_copy(layer, part, hop):
        return pltpu.make_async_remote_copy(
            src_ref=acc.at[layer, part, hop],
            dst_ref=rdp.at[layer, part, hop],
            send_sem=d_send.at[layer, part, hop],
            recv_sem=d_recv.at[layer, part, hop],
            device_id={"dp": lax.rem(dp + hop, dp_n)},
            device_id_type=MESH,
        )

    hops = list(range(1, dp_n)) + [0]
    for hop in hops:
        for layer, part in pieces:
            for shift in range(1, sub_n):
                sub_copy(layer, part, hop, shift).start()
    for hop in hops:
        chip = lax.rem(dp + hop, dp_n)
        start = pl.multiple_of((chip * sub_n + sub) * rows, rows)
        for layer, part in pieces:
            total = grad[layer, part, pl.ds(start, rows), :]
            for shift in range(1, sub_n):
                sub_copy(layer, part, hop, shift).wait()
                total = total + rsub[layer, part, hop, shift]
            acc[layer, part, hop] = total
            if hop > 0:
                dp_copy(layer, part, hop).start()
    for layer, part in pieces:
        total = acc[layer, part, 0]
        for hop in range(1, dp_n):
            dp_copy(layer, part, hop).wait()
            total = total + rdp[layer, part, hop]
        out[layer, part] = total


def wave_kernel(
    depth_n, sub_n, win, probe, counts, prop_table, far_table, delta,
    fin, mid, fout, bin_, bout, f_send, f_recv, b_send, b_recv, turn,
):
    depth, sub = lax.axis_index("depth"), lax.axis_index("sub")
    positions, layers, _, size, _ = win.shape
    is_first, is_last = depth == 0, depth == depth_n - 1
    following = lax.rem(depth + 1, depth_n)
    previous = lax.rem(depth + depth_n - 1, depth_n)
    greet([("depth", following), ("depth", previous)] + others("sub", sub_n))

    def forward_copy(item, part):
        return pltpu.make_async_remote_copy(
            src_ref=fout.at[item, part],
            dst_ref=fin.at[item, part],
            send_sem=f_send.at[item, part],
            recv_sem=f_recv.at[item, part],
            device_id={"depth": following},
            device_id_type=MESH,
        )

    def backward_copy(item):
        return pltpu.make_async_remote_copy(
            src_ref=bout.at[item],
            dst_ref=bin_.at[item],
            send_sem=b_send.at[item],
            recv_sem=b_recv.at[item],
            device_id={"depth": previous},
            device_id_type=MESH,
        )

    def forward(item):
        @pl.when(is_first)
        def _():
            fin[item] = probe[...]

        @pl.when(jnp.logical_not(is_first))
        def _():
            forward_copy(item, 0).wait_recv()
            forward_copy(item, 1).wait_recv()

        real, imag = fin[item, 0], fin[item, 1]
        for layer in range(layers):
            if layer > 0:
                mid[item, layer - 1, 0] = real
                mid[item, layer - 1, 1] = imag
            obj_re, obj_im = win[item, layer, 0], win[item, layer, 1]
            real, imag = both_sides(
                real * obj_re - imag * obj_im, real * obj_im + imag * obj_re, prop_table
            )
        fout[item, 0] = real
        fout[item, 1] = imag

        @pl.when(is_first & ((sub > 0) | (item > 0)))
        def _():
            pl.semaphore_wait(turn, 1)

        @pl.when(jnp.logical_not(is_last))
        def _():
            forward_copy(item, 0).start()
            forward_copy(item, 1).start()

        @pl.when(is_first)
        def _():
            forward_copy(item, 0).wait_send()

        @pl.when(is_first & ((sub < sub_n - 1) | (item < positions - 1)))
        def _():
            pl.semaphore_signal(
                turn, inc=1, device_id={"sub": lax.rem(sub + 1, sub_n)}, device_id_type=MESH
            )

        @pl.when(is_last)
        def _():
            far_re, far_im = both_sides(fout[item, 0], fout[item, 1], far_table)
            residual = far_re * far_re + far_im * far_im - 0.25 * counts[item].astype(jnp.float32)
            back_re, back_im = both_sides(residual * far_re, -residual * far_im, far_table)
            bin_[item, 0] = back_re
            bin_[item, 1] = back_im

    def backward(item):
        @pl.when(jnp.logical_not(is_last))
        def _():
            backward_copy(item).wait_recv()

        real, imag = bin_[item, 0], bin_[item, 1]
        for layer in reversed(range(layers)):
            real, imag = both_sides(real, imag, prop_table)
            if layer > 0:
                wave_re, wave_im = mid[item, layer - 1, 0], mid[item, layer - 1, 1]
            else:
                wave_re, wave_im = fin[item, 0], fin[item, 1]
            delta[item, layer, 0] = wave_re * real - wave_im * imag
            delta[item, layer, 1] = -(wave_re * imag + wave_im * real)
            obj_re, obj_im = win[item, layer, 0], win[item, layer, 1]
            real, imag = real * obj_re - imag * obj_im, real * obj_im + imag * obj_re

        @pl.when(jnp.logical_not(is_first))
        def _():
            bout[item, 0] = real
            bout[item, 1] = imag
            backward_copy(item).start()

    lag = 2 * (depth_n - 1 - depth)

    @pl.loop(0, positions + 2 * (depth_n - 1))
    def _(step):
        @pl.when(step < positions)
        def _():
            forward(step)

        item = step - lag

        @pl.when((item >= 0) & (item < positions))
        def _():
            backward(item)

    @pl.when(jnp.logical_not(is_last))
    def _():
        @pl.loop(0, positions)
        def _(item):
            forward_copy(item, 1).wait_send()

            @pl.when(jnp.logical_not(is_first))
            def _():
                forward_copy(item, 0).wait_send()

    @pl.when(jnp.logical_not(is_first))
    def _():
        @pl.loop(0, positions)
        def _(item):
            backward_copy(item).wait_send()


def call(body, shape, in_specs, scratch=(), collective=None):
    extra = {} if collective is None else {"collective_id": collective, "has_side_effects": True}
    return pl.pallas_call(
        body,
        out_shape=jax.ShapeDtypeStruct(shape, jnp.float32),
        in_specs=in_specs,
        out_specs=pl.BlockSpec(memory_space=pltpu.VMEM),
        scratch_shapes=list(scratch),
        compiler_params=pltpu.CompilerParams(vmem_limit_bytes=40 * 1024 * 1024, **extra),
    )


def shards(sizes, objects, probe_wave, offsets, counts):
    depth_n, dp_n, sub_n = sizes
    layers, _, half, width = objects.shape
    side = half * sub_n
    positions, size = counts.shape[0], counts.shape[1]
    rows = side // (dp_n * sub_n)
    prop_table, far_table = constants(size)
    vmem = pl.BlockSpec(memory_space=pltpu.VMEM)
    smem = pl.BlockSpec(memory_space=pltpu.SMEM)
    dma = pltpu.SemaphoreType.DMA

    def block(*shape):
        return pltpu.VMEM(shape, jnp.float32)

    full = call(
        functools.partial(gather_kernel, sub_n),
        (layers, 2, side, width),
        [vmem],
        [dma((sub_n,)), dma((sub_n,)), dma],
        0,
    )(objects)
    windows = (positions, layers, 2, size, size)
    win = call(window_kernel, windows, [smem, vmem])(offsets, full)
    waves = (positions, 2, size, size)
    delta = call(
        functools.partial(wave_kernel, depth_n, sub_n),
        windows,
        [vmem] * 5,
        [
            block(*waves),
            block(positions, max(layers - 1, 1), 2, size, size),
            block(*waves),
            block(*waves),
            block(*waves),
        ]
        + [dma((positions, 2))] * 2
        + [dma((positions,))] * 2
        + [pltpu.SemaphoreType.REGULAR],
        1,
    )(win, probe_wave, counts, jnp.asarray(prop_table), jnp.asarray(far_table))
    grad = call(scatter_kernel, (layers, 2, side + 8, width), [smem, vmem])(offsets, delta)
    return call(
        functools.partial(sum_kernel, dp_n, sub_n),
        (layers, 2, rows, width),
        [vmem],
        [
            block(layers, 2, dp_n, sub_n, rows, width),
            block(layers, 2, dp_n, rows, width),
            block(layers, 2, dp_n, rows, width),
            dma((layers, 2, dp_n, sub_n)),
            dma((layers, 2, dp_n, sub_n)),
            dma((layers, 2, dp_n)),
            dma((layers, 2, dp_n)),
        ],
        2,
    )(grad)


def solution(mesh):
    placed = (
        P(("groups", "depth"), None, "sub", None),
        P(),
        P(("groups", "dp", "sub"), None),
        P(("groups", "dp", "sub"), None, None),
    )
    sizes = tuple(mesh.shape[axis] for axis in ("depth", "dp", "sub"))
    return jax.shard_map(
        functools.partial(shards, sizes),
        mesh=mesh,
        in_specs=placed,
        out_specs=P(("groups", "depth"), None, ("dp", "sub"), None),
        check_vma=False,
    )
```

```python
import functools

import jax
import jax.numpy as jnp
import numpy as np
from jax import lax
from jax.experimental import pallas as pl
from jax.experimental.pallas import tpu as pltpu
from jax.sharding import PartitionSpec as P

KAPPA = 40.0
MESH = pl.DeviceIdType.MESH


def split_tables(matrix):
    real, imag = matrix.real, matrix.imag
    right = np.block([[real, imag], [-imag, real]]).astype(np.float32)
    tables = []
    for block in (right, right.T):
        high = block.astype(jnp.bfloat16)
        low = (block - high.astype(np.float32)).astype(jnp.bfloat16)
        tables += [high, low]
    return np.stack(tables)


def constants(size):
    index = np.arange(size)
    fourier = np.exp(-2j * np.pi * (index[:, None] * index[None, :] % size) / size)
    frequency = np.where(index < size // 2, index, index - size) / size
    ramp = np.exp(-1j * KAPPA * frequency**2)
    circulant = np.conj(fourier) @ (ramp[:, None] * fourier) / size
    circulant = 0.5 * (circulant + circulant.T)
    return split_tables(circulant), split_tables(fourier / np.sqrt(size))


def two_terms(value):
    high = value.astype(jnp.bfloat16)
    low = (value - high.astype(jnp.float32)).astype(jnp.bfloat16)
    return high, low


def dot(left, right):
    return jnp.dot(left, right, preferred_element_type=jnp.float32)


def rows_up(value, shift):
    tiles = value.reshape(value.shape[0] // 8, 8, value.shape[1])
    turned = pltpu.roll(tiles, lax.rem(8 - shift, 8), 1)
    place = lax.broadcasted_iota(jnp.int32, turned[1:].shape, 1)
    moved = jnp.where(place < 8 - shift, turned[:-1], turned[1:])
    return moved.reshape(value.shape[0] - 8, value.shape[1])


def both_sides(real, imag, table):
    size = real.shape[0]
    high, low = two_terms(jnp.concatenate([real, imag], axis=1))
    rows = dot(high, table[0]) + dot(low, table[0]) + dot(high, table[1])
    high, low = two_terms(jnp.concatenate([rows[:, :size], rows[:, size:]], axis=0))
    both = dot(table[2], high) + dot(table[2], low) + dot(table[3], high)
    return both[:size], both[size:]


def greet(neighbours):
    barrier = pltpu.get_barrier_semaphore()
    for axis, index in neighbours:
        pl.semaphore_signal(barrier, inc=1, device_id={axis: index}, device_id_type=MESH)
    pl.semaphore_wait(barrier, len(neighbours))


def others(axis, count):
    me = lax.axis_index(axis)
    return [(axis, lax.rem(me + shift, count)) for shift in range(1, count)]


def gather_kernel(sub_n, objects, full, send, recv, own_sem):
    sub = lax.axis_index("sub")
    layers, _, half, _ = objects.shape
    greet(others("sub", sub_n))
    mine = pl.ds(pl.multiple_of(sub * half, half), half)
    copies = []
    for shift in range(1, sub_n):
        copy = pltpu.make_async_remote_copy(
            src_ref=objects,
            dst_ref=full.at[:, :, mine],
            send_sem=send.at[shift],
            recv_sem=recv.at[shift],
            device_id={"sub": lax.rem(sub + shift, sub_n)},
            device_id_type=MESH,
        )
        copy.start()
        copies.append(copy)
    own = pltpu.make_async_copy(objects, full.at[:, :, mine], own_sem)
    own.start()
    own.wait()
    for copy in copies:
        copy.wait()


def window_kernel(offsets, full, win):
    positions, layers, _, size, _ = win.shape
    width = full.shape[3]

    @pl.loop(0, positions)
    def _(item):
        row, column = offsets[item, 0], offsets[item, 1]
        row_rest = lax.rem(row, 8)
        row_tile = pl.multiple_of(row - row_rest, 8)
        turn = lax.rem(width - column, width)
        for layer in range(layers):
            for part in range(2):
                strip = full[layer, part, pl.ds(row_tile, size), :]
                last = jnp.minimum(row_tile + size, full.shape[2] - 8)
                tail = full[layer, part, pl.ds(pl.multiple_of(last, 8), 8), :]
                strip = pltpu.roll(jnp.concatenate([strip, tail], axis=0), turn, 1)[:, :size]
                win[item, layer, part] = rows_up(strip, row_rest)


def scatter_kernel(offsets, delta, grad):
    positions, layers, _, size, _ = delta.shape
    width = grad.shape[3]
    grad[...] = jnp.zeros_like(grad)

    @pl.loop(0, positions)
    def _(item):
        row, column = offsets[item, 0], offsets[item, 1]
        row_rest = lax.rem(row, 8)
        row_tile = pl.multiple_of(row - row_rest, 8)
        ends = jnp.zeros((8, size), jnp.float32)
        side_by = jnp.zeros((size + 8, width - size), jnp.float32)
        for layer in range(layers):
            for part in range(2):
                tall = jnp.concatenate([ends, delta[item, layer, part], ends], axis=0)
                wide = jnp.concatenate([rows_up(tall, 8 - row_rest), side_by], axis=1)
                grad[layer, part, pl.ds(row_tile, size + 8), :] += pltpu.roll(wide, column, 1)


def sum_kernel(dp_n, sub_n, grad, out, rsub, acc, rdp, s_send, s_recv, d_send, d_recv):
    dp, sub = lax.axis_index("dp"), lax.axis_index("sub")
    layers, _, rows, _ = out.shape
    greet(others("sub", sub_n) + others("dp", dp_n))
    pieces = [(layer, part) for layer in range(layers) for part in range(2)]

    def sub_copy(layer, part, hop, shift):
        other = lax.rem(sub + shift, sub_n)
        chip = lax.rem(dp + hop, dp_n)
        start = pl.multiple_of((chip * sub_n + other) * rows, rows)
        return pltpu.make_async_remote_copy(
            src_ref=grad.at[layer, part, pl.ds(start, rows)],
            dst_ref=rsub.at[layer, part, hop, shift],
            send_sem=s_send.at[layer, part, hop, shift],
            recv_sem=s_recv.at[layer, part, hop, shift],
            device_id={"sub": other},
            device_id_type=MESH,
        )

    def dp_copy(layer, part, hop):
        return pltpu.make_async_remote_copy(
            src_ref=acc.at[layer, part, hop],
            dst_ref=rdp.at[layer, part, hop],
            send_sem=d_send.at[layer, part, hop],
            recv_sem=d_recv.at[layer, part, hop],
            device_id={"dp": lax.rem(dp + hop, dp_n)},
            device_id_type=MESH,
        )

    hops = list(range(1, dp_n)) + [0]
    for hop in hops:
        for layer, part in pieces:
            for shift in range(1, sub_n):
                sub_copy(layer, part, hop, shift).start()
    for hop in hops:
        chip = lax.rem(dp + hop, dp_n)
        start = pl.multiple_of((chip * sub_n + sub) * rows, rows)
        for layer, part in pieces:
            total = grad[layer, part, pl.ds(start, rows), :]
            for shift in range(1, sub_n):
                sub_copy(layer, part, hop, shift).wait()
                total = total + rsub[layer, part, hop, shift]
            acc[layer, part, hop] = total
            if hop > 0:
                dp_copy(layer, part, hop).start()
    for layer, part in pieces:
        total = acc[layer, part, 0]
        for hop in range(1, dp_n):
            dp_copy(layer, part, hop).wait()
            total = total + rdp[layer, part, hop]
        out[layer, part] = total


def wave_kernel(
    depth_n, win, probe, counts, tables, delta,
    waves, fout, bin_, bout, state, f_send, f_recv, b_send, b_recv,
):
    depth = lax.axis_index("depth")
    positions, layers, _, size, _ = win.shape
    is_first, is_last = depth == 0, depth == depth_n - 1
    not_first, not_last = depth > 0, depth < depth_n - 1
    following = lax.rem(depth + 1, depth_n)
    previous = lax.rem(depth + depth_n - 1, depth_n)
    greet([("depth", following), ("depth", previous)])

    def forward_copy(item):
        return pltpu.make_async_remote_copy(
            src_ref=fout.at[item],
            dst_ref=waves.at[item, 0],
            send_sem=f_send.at[item],
            recv_sem=f_recv.at[item],
            device_id={"depth": following},
            device_id_type=MESH,
        )

    def backward_copy(item):
        return pltpu.make_async_remote_copy(
            src_ref=bout.at[item],
            dst_ref=bin_.at[item],
            send_sem=b_send.at[item],
            recv_sem=b_recv.at[item],
            device_id={"depth": previous},
            device_id_type=MESH,
        )

    lag = 2 * (depth_n - 1 - depth)
    far, far_back, back = layers, layers + 1, layers + 2

    @pl.loop(0, positions + 2 * (depth_n - 1))
    def _(step):
        @pl.loop(0, 2 * layers + 2)
        def _(phase):
            is_back = phase >= back
            item = jnp.where(is_back, step - lag, step)
            is_far = (phase == far) | (phase == far_back)
            active = (item >= 0) & (item < positions) & (jnp.logical_not(is_far) | is_last)

            @pl.when(active)
            def _():
                @pl.when(phase == 0)
                def _():
                    @pl.when(is_first)
                    def _():
                        waves[item, 0] = probe[...]

                    @pl.when(not_first)
                    def _():
                        forward_copy(item).wait_recv()

                @pl.when((phase > 0) & (phase < layers))
                def _():
                    waves[item, phase] = state[...]

                @pl.when(phase < layers)
                def _():
                    real, imag = waves[item, phase, 0], waves[item, phase, 1]
                    obj_re, obj_im = win[item, phase, 0], win[item, phase, 1]
                    state[0] = real * obj_re - imag * obj_im
                    state[1] = real * obj_im + imag * obj_re

                @pl.when(phase == back)
                def _():
                    @pl.when(not_last)
                    def _():
                        backward_copy(item).wait_recv()

                    state[...] = bin_[item]

                table = tables.at[jnp.where(is_far, 1, 0)]
                real, imag = both_sides(state[0], state[1], table)
                state[0] = real
                state[1] = imag

                @pl.when((phase == layers - 1) & not_last)
                def _():
                    fout[item] = state[...]
                    forward_copy(item).start()

                @pl.when(phase == far)
                def _():
                    far_re, far_im = state[0], state[1]
                    residual = (
                        far_re * far_re + far_im * far_im - 0.25 * counts[item].astype(jnp.float32)
                    )
                    state[0] = residual * far_re
                    state[1] = -residual * far_im

                @pl.when(phase == far_back)
                def _():
                    bin_[item] = state[...]

                @pl.when(is_back)
                def _():
                    layer = 2 * layers + 1 - phase
                    real, imag = state[0], state[1]
                    wave_re, wave_im = waves[item, layer, 0], waves[item, layer, 1]
                    delta[item, layer, 0] = wave_re * real - wave_im * imag
                    delta[item, layer, 1] = -(wave_re * imag + wave_im * real)
                    obj_re, obj_im = win[item, layer, 0], win[item, layer, 1]
                    state[0] = real * obj_re - imag * obj_im
                    state[1] = real * obj_im + imag * obj_re

                    @pl.when((layer == 0) & not_first)
                    def _():
                        bout[item] = state[...]
                        backward_copy(item).start()

    @pl.when(not_last)
    def _():
        @pl.loop(0, positions)
        def _(item):
            forward_copy(item).wait_send()

    @pl.when(not_first)
    def _():
        @pl.loop(0, positions)
        def _(item):
            backward_copy(item).wait_send()


def call(body, shape, in_specs, scratch=(), collective=None):
    extra = {} if collective is None else {"collective_id": collective, "has_side_effects": True}
    return pl.pallas_call(
        body,
        out_shape=jax.ShapeDtypeStruct(shape, jnp.float32),
        in_specs=in_specs,
        out_specs=pl.BlockSpec(memory_space=pltpu.VMEM),
        scratch_shapes=list(scratch),
        compiler_params=pltpu.CompilerParams(vmem_limit_bytes=40 * 1024 * 1024, **extra),
    )


def shards(sizes, objects, probe_wave, offsets, counts):
    depth_n, dp_n, sub_n = sizes
    layers, _, half, width = objects.shape
    side = half * sub_n
    positions, size = counts.shape[0], counts.shape[1]
    rows = side // (dp_n * sub_n)
    prop_table, far_table = constants(size)
    vmem = pl.BlockSpec(memory_space=pltpu.VMEM)
    smem = pl.BlockSpec(memory_space=pltpu.SMEM)
    dma = pltpu.SemaphoreType.DMA

    def block(*shape):
        return pltpu.VMEM(shape, jnp.float32)

    full = call(
        functools.partial(gather_kernel, sub_n),
        (layers, 2, side, width),
        [vmem],
        [dma((sub_n,)), dma((sub_n,)), dma],
        0,
    )(objects)
    windows = (positions, layers, 2, size, size)
    win = call(window_kernel, windows, [smem, vmem])(offsets, full)
    waves = (positions, 2, size, size)
    delta = call(
        functools.partial(wave_kernel, depth_n),
        windows,
        [vmem] * 4,
        [block(*windows), block(*waves), block(*waves), block(*waves), block(2, size, size)]
        + [dma((positions,))] * 4,
        1,
    )(win, probe_wave, counts, jnp.asarray(np.stack([prop_table, far_table])))
    grad = call(scatter_kernel, (layers, 2, side + 8, width), [smem, vmem])(offsets, delta)
    return call(
        functools.partial(sum_kernel, dp_n, sub_n),
        (layers, 2, rows, width),
        [vmem],
        [
            block(layers, 2, dp_n, sub_n, rows, width),
            block(layers, 2, dp_n, rows, width),
            block(layers, 2, dp_n, rows, width),
            dma((layers, 2, dp_n, sub_n)),
            dma((layers, 2, dp_n, sub_n)),
            dma((layers, 2, dp_n)),
            dma((layers, 2, dp_n)),
        ],
        2,
    )(grad)


def solution(mesh):
    placed = (
        P(("groups", "depth"), None, "sub", None),
        P(),
        P(("groups", "dp", "sub"), None),
        P(("groups", "dp", "sub"), None, None),
    )
    sizes = tuple(mesh.shape[axis] for axis in ("depth", "dp", "sub"))
    return jax.shard_map(
        functools.partial(shards, sizes),
        mesh=mesh,
        in_specs=placed,
        out_specs=P(("groups", "depth"), None, ("dp", "sub"), None),
        check_vma=False,
    )
```

```python
import functools

import jax
import jax.numpy as jnp
import numpy as np
from jax import lax
from jax.experimental import pallas as pl
from jax.experimental.pallas import tpu as pltpu
from jax.sharding import PartitionSpec as P

KAPPA = 40.0
MESH = pl.DeviceIdType.MESH


def split_tables(matrix):
    real, imag = matrix.real, matrix.imag
    right = np.block([[real, imag], [-imag, real]]).astype(np.float32)
    tables = []
    for block in (right, right.T):
        high = block.astype(jnp.bfloat16)
        low = (block - high.astype(np.float32)).astype(jnp.bfloat16)
        tables += [high, low]
    return np.stack(tables)


def constants(size):
    index = np.arange(size)
    fourier = np.exp(-2j * np.pi * (index[:, None] * index[None, :] % size) / size)
    frequency = np.where(index < size // 2, index, index - size) / size
    ramp = np.exp(-1j * KAPPA * frequency**2)
    circulant = np.conj(fourier) @ (ramp[:, None] * fourier) / size
    circulant = 0.5 * (circulant + circulant.T)
    return split_tables(circulant), split_tables(fourier / np.sqrt(size))


def two_terms(value):
    high = value.astype(jnp.bfloat16)
    low = (value - high.astype(jnp.float32)).astype(jnp.bfloat16)
    return high, low


def dot(left, right):
    return jnp.dot(left, right, preferred_element_type=jnp.float32)


def rows_up(value, shift):
    tiles = value.reshape(value.shape[0] // 8, 8, value.shape[1])
    turned = pltpu.roll(tiles, lax.rem(8 - shift, 8), 1)
    place = lax.broadcasted_iota(jnp.int32, turned[1:].shape, 1)
    moved = jnp.where(place < 8 - shift, turned[:-1], turned[1:])
    return moved.reshape(value.shape[0] - 8, value.shape[1])


def both_sides(real, imag, table):
    size = real.shape[0]
    high, low = two_terms(jnp.concatenate([real, imag], axis=1))
    rows = dot(high, table[0]) + dot(low, table[0]) + dot(high, table[1])
    high, low = two_terms(jnp.concatenate([rows[:, :size], rows[:, size:]], axis=0))
    both = dot(table[2], high) + dot(table[2], low) + dot(table[3], high)
    return both[:size], both[size:]


def greet(neighbours):
    barrier = pltpu.get_barrier_semaphore()
    for axis, index in neighbours:
        pl.semaphore_signal(barrier, inc=1, device_id={axis: index}, device_id_type=MESH)
    pl.semaphore_wait(barrier, len(neighbours))


def others(axis, count):
    me = lax.axis_index(axis)
    return [(axis, lax.rem(me + shift, count)) for shift in range(1, count)]


def gather_kernel(sub_n, objects, full, send, recv, own_sem):
    sub = lax.axis_index("sub")
    layers, _, half, _ = objects.shape
    greet(others("sub", sub_n))
    mine = pl.ds(pl.multiple_of(sub * half, half), half)
    copies = []
    for shift in range(1, sub_n):
        copy = pltpu.make_async_remote_copy(
            src_ref=objects,
            dst_ref=full.at[:, :, mine],
            send_sem=send.at[shift],
            recv_sem=recv.at[shift],
            device_id={"sub": lax.rem(sub + shift, sub_n)},
            device_id_type=MESH,
        )
        copy.start()
        copies.append(copy)
    own = pltpu.make_async_copy(objects, full.at[:, :, mine], own_sem)
    own.start()
    own.wait()
    for copy in copies:
        copy.wait()


def window_kernel(offsets, full, win):
    positions, layers, _, size, _ = win.shape
    width = full.shape[3]

    @pl.loop(0, positions)
    def _(item):
        row, column = offsets[item, 0], offsets[item, 1]
        row_rest = lax.rem(row, 8)
        row_tile = pl.multiple_of(row - row_rest, 8)
        turn = lax.rem(width - column, width)
        for layer in range(layers):
            for part in range(2):
                strip = full[layer, part, pl.ds(row_tile, size), :]
                last = jnp.minimum(row_tile + size, full.shape[2] - 8)
                tail = full[layer, part, pl.ds(pl.multiple_of(last, 8), 8), :]
                strip = pltpu.roll(jnp.concatenate([strip, tail], axis=0), turn, 1)[:, :size]
                win[item, layer, part] = rows_up(strip, row_rest)


def scatter_kernel(offsets, delta, grad):
    positions, layers, _, size, _ = delta.shape
    width = grad.shape[3]
    grad[...] = jnp.zeros_like(grad)

    @pl.loop(0, positions)
    def _(item):
        row, column = offsets[item, 0], offsets[item, 1]
        row_rest = lax.rem(row, 8)
        row_tile = pl.multiple_of(row - row_rest, 8)
        ends = jnp.zeros((8, size), jnp.float32)
        side_by = jnp.zeros((size + 8, width - size), jnp.float32)
        for layer in range(layers):
            for part in range(2):
                tall = jnp.concatenate([ends, delta[item, layer, part], ends], axis=0)
                wide = jnp.concatenate([rows_up(tall, 8 - row_rest), side_by], axis=1)
                grad[layer, part, pl.ds(row_tile, size + 8), :] += pltpu.roll(wide, column, 1)


def sum_kernel(dp_n, sub_n, grad, out, rsub, acc, rdp, s_send, s_recv, d_send, d_recv):
    dp, sub = lax.axis_index("dp"), lax.axis_index("sub")
    layers, _, rows, _ = out.shape
    greet(others("sub", sub_n) + others("dp", dp_n))
    pieces = [(layer, part) for layer in range(layers) for part in range(2)]

    def sub_copy(layer, part, hop, shift):
        other = lax.rem(sub + shift, sub_n)
        chip = lax.rem(dp + hop, dp_n)
        start = pl.multiple_of((chip * sub_n + other) * rows, rows)
        return pltpu.make_async_remote_copy(
            src_ref=grad.at[layer, part, pl.ds(start, rows)],
            dst_ref=rsub.at[layer, part, hop, shift],
            send_sem=s_send.at[layer, part, hop, shift],
            recv_sem=s_recv.at[layer, part, hop, shift],
            device_id={"sub": other},
            device_id_type=MESH,
        )

    def dp_copy(layer, part, hop):
        return pltpu.make_async_remote_copy(
            src_ref=acc.at[layer, part, hop],
            dst_ref=rdp.at[layer, part, hop],
            send_sem=d_send.at[layer, part, hop],
            recv_sem=d_recv.at[layer, part, hop],
            device_id={"dp": lax.rem(dp + hop, dp_n)},
            device_id_type=MESH,
        )

    hops = list(range(1, dp_n)) + [0]
    for hop in hops:
        for layer, part in pieces:
            for shift in range(1, sub_n):
                sub_copy(layer, part, hop, shift).start()
    for hop in hops:
        chip = lax.rem(dp + hop, dp_n)
        start = pl.multiple_of((chip * sub_n + sub) * rows, rows)
        for layer, part in pieces:
            total = grad[layer, part, pl.ds(start, rows), :]
            for shift in range(1, sub_n):
                sub_copy(layer, part, hop, shift).wait()
                total = total + rsub[layer, part, hop, shift]
            acc[layer, part, hop] = total
            if hop > 0:
                dp_copy(layer, part, hop).start()
    for layer, part in pieces:
        total = acc[layer, part, 0]
        for hop in range(1, dp_n):
            dp_copy(layer, part, hop).wait()
            total = total + rdp[layer, part, hop]
        out[layer, part] = total


def wave_kernel(
    depth_n, win, probe, counts, stored_tables, delta,
    waves, fout, bin_, bout, state, tables, f_send, f_recv, b_send, b_recv, fetched,
):
    depth = lax.axis_index("depth")
    positions, layers, _, size, _ = win.shape
    is_first, is_last = depth == 0, depth == depth_n - 1
    not_first, not_last = depth > 0, depth < depth_n - 1
    following = lax.rem(depth + 1, depth_n)
    previous = lax.rem(depth + depth_n - 1, depth_n)
    fetch = pltpu.make_async_copy(stored_tables, tables, fetched)
    fetch.start()
    greet([("depth", following), ("depth", previous)])
    fetch.wait()

    def forward_copy(item):
        return pltpu.make_async_remote_copy(
            src_ref=fout.at[item],
            dst_ref=waves.at[item, 0],
            send_sem=f_send.at[item],
            recv_sem=f_recv.at[item],
            device_id={"depth": following},
            device_id_type=MESH,
        )

    def backward_copy(item):
        return pltpu.make_async_remote_copy(
            src_ref=bout.at[item],
            dst_ref=bin_.at[item],
            send_sem=b_send.at[item],
            recv_sem=b_recv.at[item],
            device_id={"depth": previous},
            device_id_type=MESH,
        )

    lag = 2 * (depth_n - 1 - depth)
    far, far_back, back = layers, layers + 1, layers + 2

    @pl.loop(0, positions + 2 * (depth_n - 1))
    def _(step):
        @pl.loop(0, 2 * layers + 2)
        def _(phase):
            is_back = phase >= back
            item = jnp.where(is_back, step - lag, step)
            is_far = (phase == far) | (phase == far_back)
            active = (item >= 0) & (item < positions) & (jnp.logical_not(is_far) | is_last)

            @pl.when(active)
            def _():
                @pl.when(phase == 0)
                def _():
                    @pl.when(is_first)
                    def _():
                        waves[item, 0] = probe[...]

                    @pl.when(not_first)
                    def _():
                        forward_copy(item).wait_recv()

                @pl.when((phase > 0) & (phase < layers))
                def _():
                    waves[item, phase] = state[...]

                @pl.when(phase < layers)
                def _():
                    real, imag = waves[item, phase, 0], waves[item, phase, 1]
                    obj_re, obj_im = win[item, phase, 0], win[item, phase, 1]
                    state[0] = real * obj_re - imag * obj_im
                    state[1] = real * obj_im + imag * obj_re

                @pl.when(phase == back)
                def _():
                    @pl.when(not_last)
                    def _():
                        backward_copy(item).wait_recv()

                    state[...] = bin_[item]

                table = tables.at[jnp.where(is_far, 1, 0)]
                real, imag = both_sides(state[0], state[1], table)
                state[0] = real
                state[1] = imag

                @pl.when((phase == layers - 1) & not_last)
                def _():
                    fout[item] = state[...]

                    @pl.when(is_first & (item > 0))
                    def _():
                        forward_copy(item - 1).wait_send()

                    forward_copy(item).start()

                @pl.when(phase == far)
                def _():
                    far_re, far_im = state[0], state[1]
                    residual = (
                        far_re * far_re + far_im * far_im - 0.25 * counts[item].astype(jnp.float32)
                    )
                    state[0] = residual * far_re
                    state[1] = -residual * far_im

                @pl.when(phase == far_back)
                def _():
                    bin_[item] = state[...]

                @pl.when(is_back)
                def _():
                    layer = 2 * layers + 1 - phase
                    real, imag = state[0], state[1]
                    obj_re, obj_im = win[item, layer, 0], win[item, layer, 1]

                    @pl.when(layer > 0)
                    def _():
                        state[0] = real * obj_re - imag * obj_im
                        state[1] = real * obj_im + imag * obj_re

                    @pl.when((layer == 0) & not_first)
                    def _():
                        bout[item, 0] = real * obj_re - imag * obj_im
                        bout[item, 1] = real * obj_im + imag * obj_re
                        backward_copy(item).start()

                    wave_re, wave_im = waves[item, layer, 0], waves[item, layer, 1]
                    delta[item, layer, 0] = wave_re * real - wave_im * imag
                    delta[item, layer, 1] = -(wave_re * imag + wave_im * real)

    @pl.when(not_last)
    def _():
        @pl.loop(0, positions)
        def _(item):
            @pl.when(not_first | (item == positions - 1))
            def _():
                forward_copy(item).wait_send()

    @pl.when(not_first)
    def _():
        @pl.loop(0, positions)
        def _(item):
            backward_copy(item).wait_send()


def call(body, shape, in_specs, scratch=(), collective=None):
    extra = {} if collective is None else {"collective_id": collective, "has_side_effects": True}
    return pl.pallas_call(
        body,
        out_shape=jax.ShapeDtypeStruct(shape, jnp.float32),
        in_specs=in_specs,
        out_specs=pl.BlockSpec(memory_space=pltpu.VMEM),
        scratch_shapes=list(scratch),
        compiler_params=pltpu.CompilerParams(vmem_limit_bytes=40 * 1024 * 1024, **extra),
    )


def shards(sizes, objects, probe_wave, offsets, counts):
    depth_n, dp_n, sub_n = sizes
    layers, _, half, width = objects.shape
    side = half * sub_n
    positions, size = counts.shape[0], counts.shape[1]
    rows = side // (dp_n * sub_n)
    tables = np.stack(constants(size))
    vmem = pl.BlockSpec(memory_space=pltpu.VMEM)
    smem = pl.BlockSpec(memory_space=pltpu.SMEM)
    dma = pltpu.SemaphoreType.DMA

    def block(*shape):
        return pltpu.VMEM(shape, jnp.float32)

    full = call(
        functools.partial(gather_kernel, sub_n),
        (layers, 2, side, width),
        [vmem],
        [dma((sub_n,)), dma((sub_n,)), dma],
        0,
    )(objects)
    windows = (positions, layers, 2, size, size)
    win = call(window_kernel, windows, [smem, vmem])(offsets, full)
    waves = (positions, 2, size, size)
    delta = call(
        functools.partial(wave_kernel, depth_n),
        windows,
        [vmem] * 3 + [pl.BlockSpec(memory_space=pl.ANY)],
        [block(*windows), block(*waves), block(*waves), block(*waves), block(2, size, size)]
        + [pltpu.VMEM(tables.shape, tables.dtype)]
        + [dma((positions,))] * 4
        + [dma],
        1,
    )(win, probe_wave, counts, jnp.asarray(tables))
    grad = call(scatter_kernel, (layers, 2, side + 8, width), [smem, vmem])(offsets, delta)
    return call(
        functools.partial(sum_kernel, dp_n, sub_n),
        (layers, 2, rows, width),
        [vmem],
        [
            block(layers, 2, dp_n, sub_n, rows, width),
            block(layers, 2, dp_n, rows, width),
            block(layers, 2, dp_n, rows, width),
            dma((layers, 2, dp_n, sub_n)),
            dma((layers, 2, dp_n, sub_n)),
            dma((layers, 2, dp_n)),
            dma((layers, 2, dp_n)),
        ],
        2,
    )(grad)


def solution(mesh):
    placed = (
        P(("groups", "depth"), None, "sub", None),
        P(),
        P(("groups", "dp", "sub"), None),
        P(("groups", "dp", "sub"), None, None),
    )
    sizes = tuple(mesh.shape[axis] for axis in ("depth", "dp", "sub"))
    return jax.shard_map(
        functools.partial(shards, sizes),
        mesh=mesh,
        in_specs=placed,
        out_specs=P(("groups", "depth"), None, ("dp", "sub"), None),
        check_vma=False,
    )
```

```python
import functools

import jax
import jax.numpy as jnp
import numpy as np
from jax import lax
from jax.experimental import pallas as pl
from jax.experimental.pallas import tpu as pltpu
from jax.sharding import PartitionSpec as P

KAPPA = 40.0
MESH = pl.DeviceIdType.MESH


def split_tables(matrix):
    real, imag = matrix.real, matrix.imag
    right = np.block([[real, imag], [-imag, real]]).astype(np.float32)
    tables = []
    for block in (right, right.T):
        high = block.astype(jnp.bfloat16)
        low = (block - high.astype(np.float32)).astype(jnp.bfloat16)
        tables += [high, low]
    return np.stack(tables)


def constants(size):
    index = np.arange(size)
    fourier = np.exp(-2j * np.pi * (index[:, None] * index[None, :] % size) / size)
    frequency = np.where(index < size // 2, index, index - size) / size
    ramp = np.exp(-1j * KAPPA * frequency**2)
    circulant = np.conj(fourier) @ (ramp[:, None] * fourier) / size
    circulant = 0.5 * (circulant + circulant.T)
    return split_tables(circulant), split_tables(fourier / np.sqrt(size))


def two_terms(value):
    high = value.astype(jnp.bfloat16)
    low = (value - high.astype(jnp.float32)).astype(jnp.bfloat16)
    return high, low


def dot(left, right):
    return jnp.dot(left, right, preferred_element_type=jnp.float32)


def rows_up(value, shift):
    tiles = value.reshape(value.shape[0] // 8, 8, value.shape[1])
    turned = pltpu.roll(tiles, lax.rem(8 - shift, 8), 1)
    place = lax.broadcasted_iota(jnp.int32, turned[1:].shape, 1)
    moved = jnp.where(place < 8 - shift, turned[:-1], turned[1:])
    return moved.reshape(value.shape[0] - 8, value.shape[1])


def both_sides(real, imag, table):
    size = real.shape[0]
    high, low = two_terms(jnp.concatenate([real, imag], axis=1))
    rows = dot(high, table[0]) + dot(low, table[0]) + dot(high, table[1])
    high, low = two_terms(jnp.concatenate([rows[:, :size], rows[:, size:]], axis=0))
    both = dot(table[2], high) + dot(table[2], low) + dot(table[3], high)
    return both[:size], both[size:]


def greet(neighbours):
    barrier = pltpu.get_barrier_semaphore()
    for axis, index in neighbours:
        pl.semaphore_signal(barrier, inc=1, device_id={axis: index}, device_id_type=MESH)
    pl.semaphore_wait(barrier, len(neighbours))


def others(axis, count):
    me = lax.axis_index(axis)
    return [(axis, lax.rem(me + shift, count)) for shift in range(1, count)]


def gather_kernel(sub_n, objects, full, send, recv, own_sem):
    sub = lax.axis_index("sub")
    layers, _, half, _ = objects.shape
    greet(others("sub", sub_n))
    mine = pl.ds(pl.multiple_of(sub * half, half), half)
    copies = []
    for shift in range(1, sub_n):
        copy = pltpu.make_async_remote_copy(
            src_ref=objects,
            dst_ref=full.at[:, :, mine],
            send_sem=send.at[shift],
            recv_sem=recv.at[shift],
            device_id={"sub": lax.rem(sub + shift, sub_n)},
            device_id_type=MESH,
        )
        copy.start()
        copies.append(copy)
    own = pltpu.make_async_copy(objects, full.at[:, :, mine], own_sem)
    own.start()
    own.wait()
    for copy in copies:
        copy.wait()


def window_kernel(offsets, full, win):
    positions, layers, _, size, _ = win.shape
    width = full.shape[3]

    @pl.loop(0, positions)
    def _(item):
        row, column = offsets[item, 0], offsets[item, 1]
        row_rest = lax.rem(row, 8)
        row_tile = pl.multiple_of(row - row_rest, 8)
        turn = lax.rem(width - column, width)
        for layer in range(layers):
            for part in range(2):
                strip = full[layer, part, pl.ds(row_tile, size), :]
                last = jnp.minimum(row_tile + size, full.shape[2] - 8)
                tail = full[layer, part, pl.ds(pl.multiple_of(last, 8), 8), :]
                strip = pltpu.roll(jnp.concatenate([strip, tail], axis=0), turn, 1)[:, :size]
                win[item, layer, part] = rows_up(strip, row_rest)


def scatter_kernel(offsets, delta, grad):
    positions, layers, _, size, _ = delta.shape
    width = grad.shape[3]
    grad[...] = jnp.zeros_like(grad)

    @pl.loop(0, positions)
    def _(item):
        row, column = offsets[item, 0], offsets[item, 1]
        row_rest = lax.rem(row, 8)
        row_tile = pl.multiple_of(row - row_rest, 8)
        ends = jnp.zeros((8, size), jnp.float32)
        side_by = jnp.zeros((size + 8, width - size), jnp.float32)
        for layer in range(layers):
            for part in range(2):
                tall = jnp.concatenate([ends, delta[item, layer, part], ends], axis=0)
                wide = jnp.concatenate([rows_up(tall, 8 - row_rest), side_by], axis=1)
                grad[layer, part, pl.ds(row_tile, size + 8), :] += pltpu.roll(wide, column, 1)


def sum_kernel(dp_n, sub_n, grad, out, rsub, acc, rdp, s_send, s_recv, d_send, d_recv):
    dp, sub = lax.axis_index("dp"), lax.axis_index("sub")
    layers, _, rows, _ = out.shape
    greet(others("sub", sub_n) + others("dp", dp_n))
    pieces = [(layer, part) for layer in range(layers) for part in range(2)]

    def sub_copy(layer, part, hop, shift):
        other = lax.rem(sub + shift, sub_n)
        chip = lax.rem(dp + hop, dp_n)
        start = pl.multiple_of((chip * sub_n + other) * rows, rows)
        return pltpu.make_async_remote_copy(
            src_ref=grad.at[layer, part, pl.ds(start, rows)],
            dst_ref=rsub.at[layer, part, hop, shift],
            send_sem=s_send.at[layer, part, hop, shift],
            recv_sem=s_recv.at[layer, part, hop, shift],
            device_id={"sub": other},
            device_id_type=MESH,
        )

    def dp_copy(layer, part, hop):
        return pltpu.make_async_remote_copy(
            src_ref=acc.at[layer, part, hop],
            dst_ref=rdp.at[layer, part, hop],
            send_sem=d_send.at[layer, part, hop],
            recv_sem=d_recv.at[layer, part, hop],
            device_id={"dp": lax.rem(dp + hop, dp_n)},
            device_id_type=MESH,
        )

    hops = list(range(1, dp_n)) + [0]
    for hop in hops:
        for layer, part in pieces:
            for shift in range(1, sub_n):
                sub_copy(layer, part, hop, shift).start()
    for hop in hops:
        chip = lax.rem(dp + hop, dp_n)
        start = pl.multiple_of((chip * sub_n + sub) * rows, rows)
        for layer, part in pieces:
            total = grad[layer, part, pl.ds(start, rows), :]
            for shift in range(1, sub_n):
                sub_copy(layer, part, hop, shift).wait()
                total = total + rsub[layer, part, hop, shift]
            acc[layer, part, hop] = total
            if hop > 0:
                dp_copy(layer, part, hop).start()
    for layer, part in pieces:
        total = acc[layer, part, 0]
        for hop in range(1, dp_n):
            dp_copy(layer, part, hop).wait()
            total = total + rdp[layer, part, hop]
        out[layer, part] = total


def wave_kernel(
    depth_n, win, probe, counts, stored_tables, delta,
    waves, fout, bin_, bout, state, tables, f_send, f_recv, b_send, b_recv, fetched,
):
    depth = lax.axis_index("depth")
    positions, layers, _, size, _ = win.shape
    is_first, is_last = depth == 0, depth == depth_n - 1
    not_first, not_last = depth > 0, depth < depth_n - 1
    following = lax.rem(depth + 1, depth_n)
    previous = lax.rem(depth + depth_n - 1, depth_n)
    fetch = pltpu.make_async_copy(stored_tables, tables, fetched)
    fetch.start()
    greet([("depth", following), ("depth", previous)])
    fetch.wait()

    def forward_copy(item):
        return pltpu.make_async_remote_copy(
            src_ref=fout.at[item],
            dst_ref=waves.at[item, 0],
            send_sem=f_send.at[item],
            recv_sem=f_recv.at[item],
            device_id={"depth": following},
            device_id_type=MESH,
        )

    def backward_copy(item):
        return pltpu.make_async_remote_copy(
            src_ref=bout.at[item],
            dst_ref=bin_.at[item],
            send_sem=b_send.at[item],
            recv_sem=b_recv.at[item],
            device_id={"depth": previous},
            device_id_type=MESH,
        )

    lag = 2 * (depth_n - 1 - depth)
    far, back = layers - 1, layers

    @pl.loop(0, positions + 2 * (depth_n - 1))
    def _(step):
        @pl.loop(0, 2 * layers)
        def _(phase):
            is_back = phase >= back
            item = jnp.where(is_back, step - lag, step)
            is_far = ((phase == far) | (phase == back)) & is_last
            active = (item >= 0) & (item < positions)

            @pl.when(active)
            def _():
                @pl.when(phase == 0)
                def _():
                    @pl.when(is_first)
                    def _():
                        waves[item, 0] = probe[...]

                    @pl.when(not_first)
                    def _():
                        forward_copy(item).wait_recv()

                @pl.when((phase > 0) & (phase < layers))
                def _():
                    waves[item, phase] = state[...]

                @pl.when(phase < layers)
                def _():
                    real, imag = waves[item, phase, 0], waves[item, phase, 1]
                    obj_re, obj_im = win[item, phase, 0], win[item, phase, 1]
                    state[0] = real * obj_re - imag * obj_im
                    state[1] = real * obj_im + imag * obj_re

                @pl.when(phase == back)
                def _():
                    @pl.when(not_last)
                    def _():
                        backward_copy(item).wait_recv()

                    state[...] = bin_[item]

                table = tables.at[jnp.where(is_far, 1, 0)]
                real, imag = both_sides(state[0], state[1], table)
                state[0] = real
                state[1] = imag

                @pl.when((phase == layers - 1) & not_last)
                def _():
                    fout[item] = state[...]

                    @pl.when(is_first & (item > 0))
                    def _():
                        forward_copy(item - 1).wait_send()

                    forward_copy(item).start()

                @pl.when((phase == far) & is_last)
                def _():
                    far_re, far_im = state[0], state[1]
                    residual = (
                        far_re * far_re + far_im * far_im - 0.25 * counts[item].astype(jnp.float32)
                    )
                    bin_[item, 0] = residual * far_re
                    bin_[item, 1] = -residual * far_im

                @pl.when(is_back)
                def _():
                    layer = 2 * layers - 1 - phase
                    real, imag = state[0], state[1]
                    obj_re, obj_im = win[item, layer, 0], win[item, layer, 1]

                    @pl.when(layer > 0)
                    def _():
                        state[0] = real * obj_re - imag * obj_im
                        state[1] = real * obj_im + imag * obj_re

                    @pl.when((layer == 0) & not_first)
                    def _():
                        bout[item, 0] = real * obj_re - imag * obj_im
                        bout[item, 1] = real * obj_im + imag * obj_re
                        backward_copy(item).start()

                    wave_re, wave_im = waves[item, layer, 0], waves[item, layer, 1]
                    delta[item, layer, 0] = wave_re * real - wave_im * imag
                    delta[item, layer, 1] = -(wave_re * imag + wave_im * real)

    @pl.when(not_last)
    def _():
        @pl.loop(0, positions)
        def _(item):
            @pl.when(not_first | (item == positions - 1))
            def _():
                forward_copy(item).wait_send()

    @pl.when(not_first)
    def _():
        @pl.loop(0, positions)
        def _(item):
            backward_copy(item).wait_send()


def call(body, shape, in_specs, scratch=(), collective=None):
    extra = {} if collective is None else {"collective_id": collective, "has_side_effects": True}
    return pl.pallas_call(
        body,
        out_shape=jax.ShapeDtypeStruct(shape, jnp.float32),
        in_specs=in_specs,
        out_specs=pl.BlockSpec(memory_space=pltpu.VMEM),
        scratch_shapes=list(scratch),
        compiler_params=pltpu.CompilerParams(vmem_limit_bytes=40 * 1024 * 1024, **extra),
    )


def shards(sizes, objects, probe_wave, offsets, counts):
    depth_n, dp_n, sub_n = sizes
    layers, _, half, width = objects.shape
    side = half * sub_n
    positions, size = counts.shape[0], counts.shape[1]
    rows = side // (dp_n * sub_n)
    tables = np.stack(constants(size))
    vmem = pl.BlockSpec(memory_space=pltpu.VMEM)
    smem = pl.BlockSpec(memory_space=pltpu.SMEM)
    dma = pltpu.SemaphoreType.DMA

    def block(*shape):
        return pltpu.VMEM(shape, jnp.float32)

    full = call(
        functools.partial(gather_kernel, sub_n),
        (layers, 2, side, width),
        [vmem],
        [dma((sub_n,)), dma((sub_n,)), dma],
        0,
    )(objects)
    windows = (positions, layers, 2, size, size)
    win = call(window_kernel, windows, [smem, vmem])(offsets, full)
    waves = (positions, 2, size, size)
    delta = call(
        functools.partial(wave_kernel, depth_n),
        windows,
        [vmem] * 3 + [pl.BlockSpec(memory_space=pl.ANY)],
        [block(*windows), block(*waves), block(*waves), block(*waves), block(2, size, size)]
        + [pltpu.VMEM(tables.shape, tables.dtype)]
        + [dma((positions,))] * 4
        + [dma],
        1,
    )(win, probe_wave, counts, jnp.asarray(tables))
    grad = call(scatter_kernel, (layers, 2, side + 8, width), [smem, vmem])(offsets, delta)
    return call(
        functools.partial(sum_kernel, dp_n, sub_n),
        (layers, 2, rows, width),
        [vmem],
        [
            block(layers, 2, dp_n, sub_n, rows, width),
            block(layers, 2, dp_n, rows, width),
            block(layers, 2, dp_n, rows, width),
            dma((layers, 2, dp_n, sub_n)),
            dma((layers, 2, dp_n, sub_n)),
            dma((layers, 2, dp_n)),
            dma((layers, 2, dp_n)),
        ],
        2,
    )(grad)


def solution(mesh):
    placed = (
        P(("groups", "depth"), None, "sub", None),
        P(),
        P(("groups", "dp", "sub"), None),
        P(("groups", "dp", "sub"), None, None),
    )
    sizes = tuple(mesh.shape[axis] for axis in ("depth", "dp", "sub"))
    return jax.shard_map(
        functools.partial(shards, sizes),
        mesh=mesh,
        in_specs=placed,
        out_specs=P(("groups", "depth"), None, ("dp", "sub"), None),
        check_vma=False,
    )
```

```python
import functools

import jax
import jax.numpy as jnp
import numpy as np
from jax import lax
from jax.experimental import pallas as pl
from jax.experimental.pallas import tpu as pltpu
from jax.sharding import PartitionSpec as P

KAPPA = 40.0
MESH = pl.DeviceIdType.MESH


def split_tables(matrix):
    real, imag = matrix.real, matrix.imag
    right = np.block([[real, imag], [-imag, real]]).astype(np.float32)
    tables = []
    for block in (right, right.T):
        high = block.astype(jnp.bfloat16)
        low = (block - high.astype(np.float32)).astype(jnp.bfloat16)
        tables += [high, low]
    return np.stack(tables)


def constants(size):
    index = np.arange(size)
    fourier = np.exp(-2j * np.pi * (index[:, None] * index[None, :] % size) / size)
    frequency = np.where(index < size // 2, index, index - size) / size
    ramp = np.exp(-1j * KAPPA * frequency**2)
    circulant = np.conj(fourier) @ (ramp[:, None] * fourier) / size
    circulant = 0.5 * (circulant + circulant.T)
    return split_tables(circulant), split_tables(fourier / np.sqrt(size))


def two_terms(value):
    high = value.astype(jnp.bfloat16)
    low = (value - high.astype(jnp.float32)).astype(jnp.bfloat16)
    return high, low


def dot(left, right):
    return jnp.dot(left, right, preferred_element_type=jnp.float32)


def rows_up(value, shift):
    tiles = value.reshape(value.shape[0] // 8, 8, value.shape[1])
    turned = pltpu.roll(tiles, lax.rem(8 - shift, 8), 1)
    place = lax.broadcasted_iota(jnp.int32, turned[1:].shape, 1)
    moved = jnp.where(place < 8 - shift, turned[:-1], turned[1:])
    return moved.reshape(value.shape[0] - 8, value.shape[1])


def both_sides(real, imag, table):
    size = real.shape[0]
    high, low = two_terms(jnp.concatenate([real, imag], axis=1))
    rows = dot(high, table[0]) + dot(low, table[0]) + dot(high, table[1])
    high, low = two_terms(jnp.concatenate([rows[:, :size], rows[:, size:]], axis=0))
    both = dot(table[2], high) + dot(table[2], low) + dot(table[3], high)
    return both[:size], both[size:]


def greet(neighbours):
    barrier = pltpu.get_barrier_semaphore()
    for axis, index in neighbours:
        pl.semaphore_signal(barrier, inc=1, device_id={axis: index}, device_id_type=MESH)
    pl.semaphore_wait(barrier, len(neighbours))


def others(axis, count):
    me = lax.axis_index(axis)
    return [(axis, lax.rem(me + shift, count)) for shift in range(1, count)]


def gather_kernel(sub_n, objects, full, send, recv, own_sem):
    sub = lax.axis_index("sub")
    layers, _, half, _ = objects.shape
    greet(others("sub", sub_n))
    mine = pl.ds(pl.multiple_of(sub * half, half), half)
    copies = []
    for shift in range(1, sub_n):
        copy = pltpu.make_async_remote_copy(
            src_ref=objects,
            dst_ref=full.at[:, :, mine],
            send_sem=send.at[shift],
            recv_sem=recv.at[shift],
            device_id={"sub": lax.rem(sub + shift, sub_n)},
            device_id_type=MESH,
        )
        copy.start()
        copies.append(copy)
    own = pltpu.make_async_copy(objects, full.at[:, :, mine], own_sem)
    own.start()
    own.wait()
    for copy in copies:
        copy.wait()


def window_kernel(offsets, full, win):
    positions, layers, _, size, _ = win.shape
    width = full.shape[3]

    @pl.loop(0, positions)
    def _(item):
        row, column = offsets[item, 0], offsets[item, 1]
        row_rest = lax.rem(row, 8)
        row_tile = pl.multiple_of(row - row_rest, 8)
        turn = lax.rem(width - column, width)
        for layer in range(layers):
            for part in range(2):
                strip = full[layer, part, pl.ds(row_tile, size), :]
                last = jnp.minimum(row_tile + size, full.shape[2] - 8)
                tail = full[layer, part, pl.ds(pl.multiple_of(last, 8), 8), :]
                strip = pltpu.roll(jnp.concatenate([strip, tail], axis=0), turn, 1)[:, :size]
                win[item, layer, part] = rows_up(strip, row_rest)


def scatter_kernel(offsets, delta, grad):
    positions, layers, _, size, _ = delta.shape
    width = grad.shape[3]
    grad[...] = jnp.zeros_like(grad)

    @pl.loop(0, positions)
    def _(item):
        row, column = offsets[item, 0], offsets[item, 1]
        row_rest = lax.rem(row, 8)
        row_tile = pl.multiple_of(row - row_rest, 8)
        ends = jnp.zeros((8, size), jnp.float32)
        side_by = jnp.zeros((size + 8, width - size), jnp.float32)
        for layer in range(layers):
            for part in range(2):
                tall = jnp.concatenate([ends, delta[item, layer, part], ends], axis=0)
                wide = jnp.concatenate([rows_up(tall, 8 - row_rest), side_by], axis=1)
                grad[layer, part, pl.ds(row_tile, size + 8), :] += pltpu.roll(wide, column, 1)


def sum_kernel(dp_n, sub_n, grad, out, rsub, acc, rdp, s_send, s_recv, d_send, d_recv):
    dp, sub = lax.axis_index("dp"), lax.axis_index("sub")
    layers, _, rows, _ = out.shape
    greet(others("sub", sub_n) + others("dp", dp_n))
    pieces = [(layer, part) for layer in range(layers) for part in range(2)]

    def sub_copy(layer, part, hop, shift):
        other = lax.rem(sub + shift, sub_n)
        chip = lax.rem(dp + hop, dp_n)
        start = pl.multiple_of((chip * sub_n + other) * rows, rows)
        return pltpu.make_async_remote_copy(
            src_ref=grad.at[layer, part, pl.ds(start, rows)],
            dst_ref=rsub.at[layer, part, hop, shift],
            send_sem=s_send.at[layer, part, hop, shift],
            recv_sem=s_recv.at[layer, part, hop, shift],
            device_id={"sub": other},
            device_id_type=MESH,
        )

    def dp_copy(layer, part, hop):
        return pltpu.make_async_remote_copy(
            src_ref=acc.at[layer, part, hop],
            dst_ref=rdp.at[layer, part, hop],
            send_sem=d_send.at[layer, part, hop],
            recv_sem=d_recv.at[layer, part, hop],
            device_id={"dp": lax.rem(dp + hop, dp_n)},
            device_id_type=MESH,
        )

    hops = list(range(1, dp_n)) + [0]
    for hop in hops:
        for layer, part in pieces:
            for shift in range(1, sub_n):
                sub_copy(layer, part, hop, shift).start()
    for hop in hops:
        chip = lax.rem(dp + hop, dp_n)
        start = pl.multiple_of((chip * sub_n + sub) * rows, rows)
        for layer, part in pieces:
            total = grad[layer, part, pl.ds(start, rows), :]
            for shift in range(1, sub_n):
                sub_copy(layer, part, hop, shift).wait()
                total = total + rsub[layer, part, hop, shift]
            acc[layer, part, hop] = total
            if hop > 0:
                dp_copy(layer, part, hop).start()
    for layer, part in pieces:
        total = acc[layer, part, 0]
        for hop in range(1, dp_n):
            dp_copy(layer, part, hop).wait()
            total = total + rdp[layer, part, hop]
        out[layer, part] = total


def wave_kernel(
    depth_n, win, probe, counts, prop_table, far_table, delta,
    waves, fout, bin_, bout, state, tables, f_send, f_recv, b_send, b_recv, fetched,
):
    depth = lax.axis_index("depth")
    positions, layers, _, size, _ = win.shape
    is_first, is_last = depth == 0, depth == depth_n - 1
    not_first, not_last = depth > 0, depth < depth_n - 1
    following = lax.rem(depth + 1, depth_n)
    previous = lax.rem(depth + depth_n - 1, depth_n)
    fetches = [
        pltpu.make_async_copy(table, tables.at[slot], fetched.at[slot])
        for slot, table in enumerate((prop_table, far_table))
    ]
    for fetch in fetches:
        fetch.start()
    greet([("depth", following), ("depth", previous)])
    for fetch in fetches:
        fetch.wait()

    def forward_copy(item):
        return pltpu.make_async_remote_copy(
            src_ref=fout.at[item],
            dst_ref=waves.at[item, 0],
            send_sem=f_send.at[item],
            recv_sem=f_recv.at[item],
            device_id={"depth": following},
            device_id_type=MESH,
        )

    def backward_copy(item):
        return pltpu.make_async_remote_copy(
            src_ref=bout.at[item],
            dst_ref=bin_.at[item],
            send_sem=b_send.at[item],
            recv_sem=b_recv.at[item],
            device_id={"depth": previous},
            device_id_type=MESH,
        )

    lag = 2 * (depth_n - 1 - depth)
    far, back = layers - 1, layers

    @pl.loop(0, positions + 2 * (depth_n - 1))
    def _(step):
        @pl.loop(0, 2 * layers)
        def _(phase):
            is_back = phase >= back
            item = jnp.where(is_back, step - lag, step)
            is_far = ((phase == far) | (phase == back)) & is_last
            active = (item >= 0) & (item < positions)

            @pl.when(active)
            def _():
                @pl.when(phase == 0)
                def _():
                    @pl.when(is_first)
                    def _():
                        waves[item, 0] = probe[...]

                    @pl.when(not_first)
                    def _():
                        forward_copy(item).wait_recv()

                @pl.when((phase > 0) & (phase < layers))
                def _():
                    waves[item, phase] = state[...]

                @pl.when(phase < layers)
                def _():
                    real, imag = waves[item, phase, 0], waves[item, phase, 1]
                    obj_re, obj_im = win[item, phase, 0], win[item, phase, 1]
                    state[0] = real * obj_re - imag * obj_im
                    state[1] = real * obj_im + imag * obj_re

                @pl.when(phase == back)
                def _():
                    @pl.when(not_last)
                    def _():
                        backward_copy(item).wait_recv()

                    state[...] = bin_[item]

                table = tables.at[jnp.where(is_far, 1, 0)]
                real, imag = both_sides(state[0], state[1], table)
                state[0] = real
                state[1] = imag

                @pl.when((phase == layers - 1) & not_last)
                def _():
                    fout[item] = state[...]

                    @pl.when(is_first & (item > 0))
                    def _():
                        forward_copy(item - 1).wait_send()

                    forward_copy(item).start()

                @pl.when((phase == far) & is_last)
                def _():
                    far_re, far_im = state[0], state[1]
                    residual = (
                        far_re * far_re + far_im * far_im - 0.25 * counts[item].astype(jnp.float32)
                    )
                    bin_[item, 0] = residual * far_re
                    bin_[item, 1] = -residual * far_im

                @pl.when(is_back)
                def _():
                    layer = 2 * layers - 1 - phase
                    real, imag = state[0], state[1]
                    obj_re, obj_im = win[item, layer, 0], win[item, layer, 1]

                    @pl.when(layer > 0)
                    def _():
                        state[0] = real * obj_re - imag * obj_im
                        state[1] = real * obj_im + imag * obj_re

                    @pl.when((layer == 0) & not_first)
                    def _():
                        bout[item, 0] = real * obj_re - imag * obj_im
                        bout[item, 1] = real * obj_im + imag * obj_re
                        backward_copy(item).start()

                    wave_re, wave_im = waves[item, layer, 0], waves[item, layer, 1]
                    delta[item, layer, 0] = wave_re * real - wave_im * imag
                    delta[item, layer, 1] = -(wave_re * imag + wave_im * real)

    @pl.when(not_last)
    def _():
        @pl.loop(0, positions)
        def _(item):
            @pl.when(not_first | (item == positions - 1))
            def _():
                forward_copy(item).wait_send()

    @pl.when(not_first)
    def _():
        @pl.loop(0, positions)
        def _(item):
            backward_copy(item).wait_send()


def call(body, shape, in_specs, scratch=(), collective=None):
    extra = {} if collective is None else {"collective_id": collective, "has_side_effects": True}
    return pl.pallas_call(
        body,
        out_shape=jax.ShapeDtypeStruct(shape, jnp.float32),
        in_specs=in_specs,
        out_specs=pl.BlockSpec(memory_space=pltpu.VMEM),
        scratch_shapes=list(scratch),
        compiler_params=pltpu.CompilerParams(vmem_limit_bytes=40 * 1024 * 1024, **extra),
    )


def shards(sizes, objects, probe_wave, offsets, counts):
    depth_n, dp_n, sub_n = sizes
    layers, _, half, width = objects.shape
    side = half * sub_n
    positions, size = counts.shape[0], counts.shape[1]
    rows = side // (dp_n * sub_n)
    tables = np.stack(constants(size))
    vmem = pl.BlockSpec(memory_space=pltpu.VMEM)
    smem = pl.BlockSpec(memory_space=pltpu.SMEM)
    dma = pltpu.SemaphoreType.DMA

    def block(*shape):
        return pltpu.VMEM(shape, jnp.float32)

    full = call(
        functools.partial(gather_kernel, sub_n),
        (layers, 2, side, width),
        [vmem],
        [dma((sub_n,)), dma((sub_n,)), dma],
        0,
    )(objects)
    windows = (positions, layers, 2, size, size)
    win = call(window_kernel, windows, [smem, vmem])(offsets, full)
    waves = (positions, 2, size, size)
    delta = call(
        functools.partial(wave_kernel, depth_n),
        windows,
        [vmem] * 3 + [pl.BlockSpec(memory_space=pl.ANY)] * 2,
        [block(*windows), block(*waves), block(*waves), block(*waves), block(2, size, size)]
        + [pltpu.VMEM(tables.shape, tables.dtype)]
        + [dma((positions,))] * 4
        + [dma((2,))],
        1,
    )(win, probe_wave, counts, jnp.asarray(tables[0]), jnp.asarray(tables[1]))
    grad = call(scatter_kernel, (layers, 2, side + 8, width), [smem, vmem])(offsets, delta)
    return call(
        functools.partial(sum_kernel, dp_n, sub_n),
        (layers, 2, rows, width),
        [vmem],
        [
            block(layers, 2, dp_n, sub_n, rows, width),
            block(layers, 2, dp_n, rows, width),
            block(layers, 2, dp_n, rows, width),
            dma((layers, 2, dp_n, sub_n)),
            dma((layers, 2, dp_n, sub_n)),
            dma((layers, 2, dp_n)),
            dma((layers, 2, dp_n)),
        ],
        2,
    )(grad)


def solution(mesh):
    placed = (
        P(("groups", "depth"), None, "sub", None),
        P(),
        P(("groups", "dp", "sub"), None),
        P(("groups", "dp", "sub"), None, None),
    )
    sizes = tuple(mesh.shape[axis] for axis in ("depth", "dp", "sub"))
    return jax.shard_map(
        functools.partial(shards, sizes),
        mesh=mesh,
        in_specs=placed,
        out_specs=P(("groups", "depth"), None, ("dp", "sub"), None),
        check_vma=False,
    )
```
